128 devices in a mesh: gx: 8 (over z, core), yz: 16 (over x, y).
Axes of the slice: x: 4, y: 4, z: 4, core: 2. Of those that a mesh axis runs over, the one named last changes fastest.
Arguments:
- resid: bfloat16 [512, 16384], P(None, 'gx'), may hold values from -6 to 6
- queries: bfloat16 [512, 8192], P(None, 'yz'), may hold values from -128 to 128
- new_keys: bfloat16 [512, 512], P(None, 'yz'), may hold values from -4.5 to 4.5
- new_values: bfloat16 [512, 512], P(None, 'yz'), may hold values from -5 to 5
- cache_keys: bfloat16 [512, 384, 512], P(('gx', 'yz')), may hold values from -4.5 to 4.5
- cache_values: bfloat16 [512, 384, 512], P(('gx', 'yz')), may hold values from -5 to 5
- lengths: int32 [512], replicated, may hold values from 1 to 384, as said below
- cache_slot: int32 [512], replicated, may hold values from 0 to 511, as said below
- out_weight: bfloat16 [8192, 16384], P('yz', 'gx'), may hold values from -0.0625 to 0.0625
- norm_gain: float32 [16384], P('gx'), may hold values from 0.1 to 1.9
- gate_weight: bfloat16 [16384, 28672], P('gx', 'yz'), may hold values from -0.046875 to 0.046875
- up_weight: bfloat16 [16384, 28672], P('gx', 'yz'), may hold values from -0.046875 to 0.046875
- down_weight: bfloat16 [28672, 16384], P('yz', 'gx'), may hold values from -0.03125 to 0.03125
Outputs:
- layer_out: bfloat16 [512, 16384], P('yz', 'gx')
The draws below stay inside these ranges and needn't reach their ends.
Inputs may be any that keep to these rules, and one draw needn't show every extreme that they name: `cache_slot`: each slot number appears once; slot s lies on the device of index s // 4 along gx+yz. `lengths`: cache positions at or past a row's length hold entries that are not part of its context.
All inputs are finite; a program needn't handle non-finite values.
Results may differ from the reference program's by a relative error of at most 0.015.
Values may be sent and summed in bfloat16 or wider, within the bound.
No kernel may reach another device: no remote copies, remote signals or barrier semaphores. Data moves between devices by JAX's collectives and lax.ppermute only.
A program may use at most 128 MiB of HBM per device.

```python
import math
from functools import partial
import jax
import jax.numpy as jnp
from jax import lax

D = 16384
FF = 28672
QH = 64
KVH = 4
HD = 128
CTX = 384
ROWS = 512


def shared_routing(key):
    key = jax.random.fold_in(key, 11)
    first, second, third, fourth = jax.random.split(key, 4)
    slots = jax.random.permutation(first, ROWS).astype(jnp.int32)
    draw_one = jax.random.randint(second, (ROWS,), 1, CTX + 1)
    draw_two = jax.random.randint(third, (ROWS,), 1, CTX + 1)
    valid = jnp.minimum(draw_one, draw_two)
    longest = jax.random.randint(fourth, (), 0, ROWS)
    valid = jnp.where(jnp.arange(ROWS) == longest, CTX, valid).astype(jnp.int32)
    return (slots, valid)


def shared_keys(key):
    key = jax.random.fold_in(key, 23)
    return jnp.clip(jax.random.normal(key, (ROWS, KVH * HD), jnp.float32), -4.5, 4.5)


def draw_cache_slot(key, part):
    return shared_routing(key)[0]


def draw_lengths(key, part):
    return shared_routing(key)[1]


def draw_new_keys(key, part):
    return shared_keys(key).astype(jnp.bfloat16)


def draw_queries(key, part):
    key = jax.random.fold_in(key, 3)
    first, second = jax.random.split(key)
    scales = jnp.exp(jax.random.uniform(second, (ROWS, 1), jnp.float32, math.log(0.3), math.log(3.0)))
    return (jnp.clip(jax.random.normal(first, (ROWS, QH * HD), jnp.float32), -4.5, 4.5) * scales).astype(jnp.bfloat16)


def draw_cache_keys(key, part):
    key = jax.random.fold_in(key, 5)
    return jnp.clip(jax.random.normal(key, (ROWS, CTX, KVH * HD), jnp.float32), -4.5, 4.5).astype(jnp.bfloat16)


def levels(rng, shape, pieces, low, high):
    loudness = 1.0
    for position, shards_of in pieces:
        steps = jax.random.uniform(jax.random.fold_in(jax.random.fold_in(rng, 6), position), (shards_of,), jnp.float32, low / len(pieces), high / len(pieces))
        loudness = loudness * jnp.repeat(jnp.exp(steps), shape[position] // shards_of).reshape((-1,) + (1,) * (len(shape) - 1 - position))
    return loudness


def gaussian(key, dims, width, limit, cuts=(), held_as=jnp.bfloat16):
    array = jax.random.normal(key, dims, jnp.float32) * width
    if len(cuts) > 0:
        array = levels(key, dims, cuts, -0.22, 0.18) * array
    return jnp.clip(array, min=-limit, max=limit).astype(held_as)


def setup_inputs(seed: int = 0) -> dict:
    splits = jax.random.split(jax.random.key(seed), 14)
    resid = gaussian(splits[0], (ROWS, D), 1.0, 6.0, ((1, 8),))
    queries = draw_queries(jax.random.fold_in(splits[13], 71), 0)
    new_keys = draw_new_keys(jax.random.fold_in(splits[13], 71), 0)
    new_values = gaussian(splits[3], (ROWS, KVH * HD), 1.0, 5.0, ((1, 16),))
    cache_keys = draw_cache_keys(jax.random.fold_in(splits[13], 71), 0)
    cache_values = gaussian(splits[5], (ROWS, CTX, KVH * HD), 1.0, 5.0, ((0, 128),))
    lengths = draw_lengths(jax.random.fold_in(splits[13], 71), 0)
    cache_slot = draw_cache_slot(jax.random.fold_in(splits[13], 71), 0)
    out_weight = gaussian(splits[8], (QH * HD, D), (QH * HD) ** -0.5, 0.0625, ((0, 16), (1, 8)))
    norm_gain = jnp.clip(1.0 + 0.18 * jax.random.normal(splits[9], (D,), jnp.float32), 0.1, 1.9)
    gate_weight = gaussian(splits[10], (D, FF), D ** -0.5, 0.046875, ((0, 8), (1, 16)))
    up_weight = gaussian(splits[11], (D, FF), D ** -0.5, 0.046875, ((0, 8), (1, 16)))
    down_weight = gaussian(splits[12], (FF, D), FF ** -0.5, 0.03125, ((0, 16), (1, 8)))
    return {"resid": resid, "queries": queries, "new_keys": new_keys, "new_values": new_values, "cache_keys": cache_keys, "cache_values": cache_values, "lengths": lengths, "cache_slot": cache_slot, "out_weight": out_weight, "norm_gain": norm_gain, "gate_weight": gate_weight, "up_weight": up_weight, "down_weight": down_weight}


def attend_row(cache_keys, cache_values, operands):
    query, key_new, value_new, slot_id, valid = operands
    groups = QH // KVH
    keys = lax.dynamic_index_in_dim(cache_keys, slot_id, 0, keepdims=False)
    values = lax.dynamic_index_in_dim(cache_values, slot_id, 0, keepdims=False)
    query_heads = query.reshape(KVH, groups, HD).astype(jnp.float32)
    key_heads = keys.reshape(CTX, KVH, HD).astype(jnp.float32)
    value_heads = values.reshape(CTX, KVH, HD).astype(jnp.float32)
    scaling = HD ** (-0.5)
    scores = jnp.einsum('kgd,ckd->kgc', query_heads, key_heads) * scaling
    new_score = jnp.einsum('kgd,kd->kg', query_heads, key_new.reshape(KVH, HD).astype(jnp.float32)) * scaling
    inside = jnp.arange(CTX) < valid
    scores = jnp.where(inside[None, None, :], scores, -jnp.inf)
    largest = jnp.maximum(lax.optimization_barrier(jnp.max(scores, axis=-1)), new_score)
    powers = jnp.exp(scores - largest[..., None])
    power_new = jnp.exp(new_score - largest)
    totals = lax.optimization_barrier(jnp.sum(powers, axis=-1)) + power_new
    weights = (powers / totals[..., None]).astype(jnp.bfloat16)
    weight_new = (power_new / totals).astype(jnp.bfloat16)
    context = jnp.einsum('kgc,ckd->kgd', weights.astype(jnp.float32), value_heads)
    context = context + weight_new.astype(jnp.float32)[..., None] * value_new.reshape(KVH, 1, HD).astype(jnp.float32)
    return context.reshape(QH * HD).astype(jnp.bfloat16)

def reference(resid, queries, new_keys, new_values, cache_keys, cache_values, lengths, cache_slot, out_weight, norm_gain, gate_weight, up_weight, down_weight):
    context = lax.map(partial(attend_row, cache_keys, cache_values), (queries, new_keys, new_values, cache_slot.astype(jnp.int32), lengths.astype(jnp.int32)))
    attended = jnp.dot(context, out_weight, preferred_element_type=jnp.float32)
    middle = (resid.astype(jnp.float32) + attended).astype(jnp.bfloat16)
    mid_float = middle.astype(jnp.float32)
    mean_square = lax.optimization_barrier(jnp.mean(mid_float * mid_float, axis=1))
    normed = (mid_float * lax.rsqrt(mean_square + 1e-05)[:, None] * norm_gain.astype(jnp.float32)[None, :]).astype(jnp.bfloat16)
    gate = jnp.dot(normed, gate_weight, preferred_element_type=jnp.float32)
    upper = jnp.dot(normed, up_weight, preferred_element_type=jnp.float32)
    hidden = (jax.nn.silu(gate) * upper).astype(jnp.bfloat16)
    projected = jnp.dot(hidden, down_weight, preferred_element_type=jnp.float32)
    return (mid_float + projected).astype(jnp.bfloat16)
```

```python
import jax
import jax.numpy as jnp
from jax import lax
from jax.sharding import PartitionSpec as P

HD = 128
RING = 4
CORES = 2
AXES = ("gx", "yz")
BF16 = jnp.bfloat16
F32 = jnp.float32
FAR_FIRST = (2, 1, 3, 0)


def place(device):
    gx, yz = divmod(device, RING * RING)
    z, core = divmod(gx, CORES)
    x, y = divmod(yz, RING)
    return x, y, z, core


def number(x, y, z, core):
    gx = (z % RING) * CORES + core
    return gx * RING * RING + (x % RING) * RING + y % RING


def pairs(move):
    count = RING * RING * RING * CORES
    return [(d, number(*move(*place(d)))) for d in range(count)]


def send_first(value, step):
    def move(x, y, z, core):
        return (x + step, y, z, core) if core == 0 else (x, y + step, z, core)

    return lax.ppermute(value, AXES, pairs(move))


def send_second(value, step):
    def move(x, y, z, core):
        return (x, y + step, z, core) if core == 0 else (x + step, y, z, core)

    return lax.ppermute(value, AXES, pairs(move))


def send_z(value, step):
    return lax.ppermute(value, AXES, pairs(lambda x, y, z, core: (x, y, z + step, core)))


def send_core(value):
    return lax.ppermute(value, AXES, pairs(lambda x, y, z, core: (x, y, z, 1 - core)))


def spread(send, blocks):
    return [send(blocks[j], j) for j in FAR_FIRST if j != 0]


def collect(send, value):
    got = {0: value}
    for j in (2, 1, 3):
        got[j] = send(value, -j)
    return [got[j] for j in range(RING)]


def add_up(own, others):
    total = own.astype(F32)
    for other in others:
        total = total + other.astype(F32)
    return total


def hi_lo(total):
    high = lax.reduce_precision(total, exponent_bits=8, mantissa_bits=7)
    return high.astype(BF16), (total - high).astype(BF16)


def one_hot_rows(index, count):
    return (index[:, None] == jnp.arange(count, dtype=jnp.int32)[None, :]).astype(BF16)


def pick(matrix, values):
    return jnp.dot(matrix, values, preferred_element_type=F32).astype(BF16)


def attend_slots(query_heads, key_rows, value_rows, cache_keys, cache_values, valid):
    slot_count, positions = cache_keys.shape[:2]
    kv_heads, groups = query_heads.shape[1:3]
    scaling = HD ** (-0.5)
    key_heads = cache_keys.reshape(slot_count, positions, kv_heads, HD)
    value_heads = cache_values.reshape(slot_count, positions, kv_heads, HD)
    scores = (
        jnp.einsum("bkgd,bckd->bkgc", query_heads, key_heads, preferred_element_type=F32) * scaling
    )
    new_score = (
        jnp.einsum("bkgd,bkd->bkg", query_heads, key_rows, preferred_element_type=F32) * scaling
    )
    inside = jnp.arange(positions)[None, :] < valid[:, None]
    scores = jnp.where(inside[:, None, None, :], scores, -jnp.inf)
    largest = jnp.maximum(jnp.max(scores, axis=-1), new_score)
    powers = jnp.exp(scores - largest[..., None])
    power_new = jnp.exp(new_score - largest)
    totals = jnp.sum(powers, axis=-1) + power_new
    weights = (powers / totals[..., None]).astype(BF16)
    weight_new = (power_new / totals).astype(BF16)
    context = jnp.einsum("bkgc,bckd->bkgd", weights, value_heads, preferred_element_type=F32)
    context = context + weight_new.astype(F32)[..., None] * value_rows.astype(F32)[:, :, None, :]
    return context.reshape(slot_count, kv_heads * groups * HD).astype(BF16)


def on_device(
    resid,
    queries,
    new_keys,
    new_values,
    cache_keys,
    cache_values,
    lengths,
    cache_slot,
    out_weight,
    norm_gain,
    gate_weight,
    up_weight,
    down_weight,
):
    index_gx = lax.axis_index("gx")
    index_yz = lax.axis_index("yz")
    count_yz = RING * RING
    count_gx = RING * CORES
    z, core = index_gx // CORES, index_gx % CORES
    x, y = index_yz // RING, index_yz % RING
    rows = resid.shape[0]
    width = resid.shape[1]
    hidden_width = gate_weight.shape[1]
    per_device = cache_keys.shape[0]
    group_slots = per_device * count_yz
    block = rows // count_yz
    kv_heads = cache_keys.shape[2] // HD
    head_width = out_weight.shape[0]
    heads_here = head_width // HD
    new_width = new_keys.shape[1]
    positions = jnp.arange(rows, dtype=jnp.int32)

    slot_here = index_gx * group_slots + jnp.arange(group_slots, dtype=jnp.int32)
    routing = cache_slot[None, :] == slot_here[:, None]
    outgoing = pick(
        routing.astype(BF16), jnp.concatenate([queries, new_keys, new_values], axis=1)
    )
    valid = jnp.sum(jnp.where(routing, lengths[None, :], 0), axis=1)
    valid_own = lax.dynamic_slice_in_dim(valid, index_yz * per_device, per_device)
    arrived = lax.all_to_all(outgoing, "yz", split_axis=0, concat_axis=0, tiled=True)
    arrived = arrived.reshape(count_yz, per_device, head_width + 2 * new_width)
    query_heads = (
        arrived[:, :, :head_width]
        .reshape(count_yz, per_device, heads_here, HD)
        .transpose(1, 0, 2, 3)
        .reshape(per_device, kv_heads, count_yz * heads_here // kv_heads, HD)
    )
    key_rows = (
        arrived[:, :, head_width : head_width + new_width]
        .transpose(1, 0, 2)
        .reshape(per_device, kv_heads, HD)
    )
    value_rows = (
        arrived[:, :, head_width + new_width :].transpose(1, 0, 2).reshape(per_device, kv_heads, HD)
    )
    context = attend_slots(query_heads, key_rows, value_rows, cache_keys, cache_values, valid_own)

    columns = lax.all_to_all(
        context.reshape(per_device, count_yz, head_width).transpose(1, 0, 2),
        "yz",
        split_axis=0,
        concat_axis=0,
        tiled=True,
    ).reshape(group_slots, head_width)
    own_columns = jnp.concatenate(collect(send_z, columns), axis=0)
    all_columns = jnp.concatenate([own_columns, send_core(own_columns)], axis=0)
    order = jnp.arange(count_gx * group_slots, dtype=jnp.int32)
    order_core = (order // (RING * group_slots) + core) % CORES
    order_z = (order // group_slots + z) % RING
    order_slot = (order_z * CORES + order_core) * group_slots + order % group_slots

    far, near, inner = positions // (RING * block), (positions // block) % RING, positions % block
    row_x = jnp.where(core == 0, x + far, x + near) % RING
    row_y = jnp.where(core == 0, y + near, y + far) % RING
    row_here = (row_x * RING + row_y) * block + inner
    slot_of = jnp.sum(
        jnp.where(row_here[:, None] == positions[None, :], cache_slot[None, :], 0), axis=1
    )
    context_rows = pick((slot_of[:, None] == order_slot[None, :]).astype(BF16), all_columns)

    def sum_rows(product):
        chunk = RING * block
        parts = {}
        for j in FAR_FIRST:
            part = product(slice(j * chunk, (j + 1) * chunk))
            parts[j] = part if j == 0 else part.astype(BF16)
        total = add_up(parts[0], spread(send_first, parts))
        parts = {k: total[k * block : (k + 1) * block] for k in range(RING)}
        parts = {k: part if k == 0 else part.astype(BF16) for k, part in parts.items()}
        return add_up(parts[0], spread(send_second, parts))

    attended = sum_rows(
        lambda part: jnp.dot(context_rows[part], out_weight, preferred_element_type=F32)
    )
    own_resid = lax.dynamic_slice_in_dim(resid, index_yz * block, block, 0)
    middle = (own_resid.astype(F32) + attended).astype(BF16)
    mid_float = middle.astype(F32)
    scaled = (mid_float * norm_gain[None, :]).astype(BF16)
    high, low = hi_lo(jnp.sum(mid_float * mid_float, axis=1, keepdims=True))
    tail = [jnp.broadcast_to(part, (block, HD // 2)) for part in (high, low)]
    payload = jnp.concatenate([scaled] + tail, axis=1)

    blocks = jnp.concatenate(collect(send_second, payload), axis=0)
    blocks = jnp.concatenate(collect(send_first, blocks), axis=0)

    half = RING * block // CORES
    target = (positions // (RING * block)) % RING
    along = jnp.asarray(FAR_FIRST, jnp.int32)
    distance = jnp.sum(jnp.where(target[:, None] == jnp.arange(RING)[None, :], along[None, :], 0), axis=1)
    part_x = (z + distance) % RING
    part_core = jnp.where((positions // half) % CORES == 0, 1 - core, core)
    part_y = part_core * (RING // CORES) + (positions // block) % (RING // CORES)
    source = jnp.where(core == 0, part_x * RING + part_y, part_y * RING + part_x) * block + inner
    sorted_rows = pick(one_hot_rows(source, rows), blocks)

    parts = {}
    for order_index, j in enumerate(FAR_FIRST):
        chunk = sorted_rows[order_index * RING * block : (order_index + 1) * RING * block]
        gate = jnp.dot(chunk[:, :width], gate_weight, preferred_element_type=F32)
        upper = jnp.dot(chunk[:, :width], up_weight, preferred_element_type=F32)
        squares = chunk[:, width:]
        other = send_core(
            jnp.concatenate(
                [gate[:half].astype(BF16), upper[:half].astype(BF16), squares[:half]], axis=1
            )
        )
        both_gate = gate[half:] + other[:, :hidden_width].astype(F32)
        both_upper = upper[half:] + other[:, hidden_width : 2 * hidden_width].astype(F32)
        both_squares = add_up(squares[half:], [other[:, 2 * hidden_width :]])
        both_squares = both_squares[:, :1] + both_squares[:, HD // 2 : HD // 2 + 1]
        if j == 0:
            parts[j] = (both_gate, both_upper, both_squares)
        else:
            tail = [jnp.broadcast_to(p, (half, HD // 2)) for p in hi_lo(both_squares)]
            parts[j] = jnp.concatenate(
                [both_gate.astype(BF16), both_upper.astype(BF16)] + tail, axis=1
            )
    others = spread(send_z, parts)
    gate = add_up(parts[0][0], [o[:, :hidden_width] for o in others])
    upper = add_up(parts[0][1], [o[:, hidden_width : 2 * hidden_width] for o in others])
    ends = [o[:, 2 * hidden_width :] for o in others]
    squares = add_up(
        parts[0][2], [e[:, :1] for e in ends] + [e[:, HD // 2 : HD // 2 + 1] for e in ends]
    )
    factor = lax.rsqrt(squares / (width * count_gx) + 1e-05)
    gate = gate * factor
    hidden = (jax.nn.silu(gate) * (upper * factor)).astype(BF16)

    own_hidden = collect(send_z, hidden)
    other_hidden = [send_core(part) for part in own_hidden]
    all_hidden = jnp.concatenate(own_hidden + other_hidden, axis=0)
    place_x = jnp.where(core == 0, far, near)
    place_y = jnp.where(core == 0, near, far)
    place_core = (place_y // (RING // CORES) + core) % CORES
    place_z = (place_x - z) % RING
    place_here = (place_core * RING + place_z) * half + (place_y % (RING // CORES)) * block + inner
    hidden_rows = pick(one_hot_rows(place_here, rows), all_hidden)
    projected = sum_rows(
        lambda part: jnp.dot(hidden_rows[part], down_weight, preferred_element_type=F32)
    )
    return (mid_float + projected).astype(BF16)


def solution(mesh):
    in_specs = (
        P(None, "gx"),
        P(None, "yz"),
        P(None, "yz"),
        P(None, "yz"),
        P(("gx", "yz"), None, None),
        P(("gx", "yz"), None, None),
        P(),
        P(),
        P("yz", "gx"),
        P("gx"),
        P("gx", "yz"),
        P("gx", "yz"),
        P("yz", "gx"),
    )
    out_specs = P("yz", "gx")
    return jax.shard_map(
        on_device, mesh=mesh, in_specs=in_specs, out_specs=out_specs, check_vma=False
    )
```

```python
import jax
import jax.numpy as jnp
from jax import lax
from jax.sharding import PartitionSpec as P

HD = 128
RING = 4
CORES = 2
AXES = ("gx", "yz")
BF16 = jnp.bfloat16
F32 = jnp.float32
FAR_FIRST = (2, 1, 3, 0)


def place(device):
    gx, yz = divmod(device, RING * RING)
    z, core = divmod(gx, CORES)
    x, y = divmod(yz, RING)
    return x, y, z, core


def number(x, y, z, core):
    gx = (z % RING) * CORES + core
    return gx * RING * RING + (x % RING) * RING + y % RING


def pairs(move):
    count = RING * RING * RING * CORES
    return [(d, number(*move(*place(d)))) for d in range(count)]


def send_first(value, step):
    def move(x, y, z, core):
        return (x + step, y, z, core) if core == 0 else (x, y + step, z, core)

    return lax.ppermute(value, AXES, pairs(move))


def send_second(value, step):
    def move(x, y, z, core):
        return (x, y + step, z, core) if core == 0 else (x + step, y, z, core)

    return lax.ppermute(value, AXES, pairs(move))


def send_z(value, step):
    return lax.ppermute(value, AXES, pairs(lambda x, y, z, core: (x, y, z + step, core)))


def send_core(value):
    return lax.ppermute(value, AXES, pairs(lambda x, y, z, core: (x, y, z, 1 - core)))


def spread(send, blocks):
    return [send(blocks[j], j) for j in FAR_FIRST if j != 0]


def collect(send, value):
    got = {0: value}
    for j in (2, 1, 3):
        got[j] = send(value, -j)
    return [got[j] for j in range(RING)]


def add_up(own, others):
    total = own.astype(F32)
    for other in others:
        total = total + other.astype(F32)
    return total


def hi_lo(total):
    high = lax.reduce_precision(total, exponent_bits=8, mantissa_bits=7)
    return high.astype(BF16), (total - high).astype(BF16)


def one_hot_rows(index, count):
    return (index[:, None] == jnp.arange(count, dtype=jnp.int32)[None, :]).astype(BF16)


def pick(matrix, values):
    return jnp.dot(matrix, values, preferred_element_type=F32).astype(BF16)


def attend_slots(query_heads, key_rows, value_rows, cache_keys, cache_values, valid):
    slot_count, positions = cache_keys.shape[:2]
    kv_heads, groups = query_heads.shape[1:3]
    scaling = HD ** (-0.5)
    key_heads = cache_keys.reshape(slot_count, positions, kv_heads, HD)
    value_heads = cache_values.reshape(slot_count, positions, kv_heads, HD)
    scores = (
        jnp.einsum("bkgd,bckd->bkgc", query_heads, key_heads, preferred_element_type=F32) * scaling
    )
    new_score = (
        jnp.einsum("bkgd,bkd->bkg", query_heads, key_rows, preferred_element_type=F32) * scaling
    )
    inside = jnp.arange(positions)[None, :] < valid[:, None]
    scores = jnp.where(inside[:, None, None, :], scores, -jnp.inf)
    largest = jnp.maximum(jnp.max(scores, axis=-1), new_score)
    powers = jnp.exp(scores - largest[..., None])
    power_new = jnp.exp(new_score - largest)
    totals = jnp.sum(powers, axis=-1) + power_new
    weights = (powers / totals[..., None]).astype(BF16)
    weight_new = (power_new / totals).astype(BF16)
    context = jnp.einsum("bkgc,bckd->bkgd", weights, value_heads, preferred_element_type=F32)
    context = context + weight_new.astype(F32)[..., None] * value_rows.astype(F32)[:, :, None, :]
    return context.reshape(slot_count, kv_heads * groups * HD).astype(BF16)


def on_device(
    resid,
    queries,
    new_keys,
    new_values,
    cache_keys,
    cache_values,
    lengths,
    cache_slot,
    out_weight,
    norm_gain,
    gate_weight,
    up_weight,
    down_weight,
):
    index_gx = lax.axis_index("gx")
    index_yz = lax.axis_index("yz")
    count_yz = RING * RING
    count_gx = RING * CORES
    z, core = index_gx // CORES, index_gx % CORES
    x, y = index_yz // RING, index_yz % RING
    rows = resid.shape[0]
    width = resid.shape[1]
    hidden_width = gate_weight.shape[1]
    per_device = cache_keys.shape[0]
    group_slots = per_device * count_yz
    block = rows // count_yz
    kv_heads = cache_keys.shape[2] // HD
    head_width = out_weight.shape[0]
    heads_here = head_width // HD
    new_width = new_keys.shape[1]
    positions = jnp.arange(rows, dtype=jnp.int32)

    slot_here = index_gx * group_slots + jnp.arange(group_slots, dtype=jnp.int32)
    routing = cache_slot[None, :] == slot_here[:, None]
    outgoing = pick(
        routing.astype(BF16), jnp.concatenate([queries, new_keys, new_values], axis=1)
    )
    valid = jnp.sum(jnp.where(routing, lengths[None, :], 0), axis=1)
    valid_own = lax.dynamic_slice_in_dim(valid, index_yz * per_device, per_device)
    arrived = lax.all_to_all(outgoing, "yz", split_axis=0, concat_axis=0, tiled=True)
    arrived = arrived.reshape(count_yz, per_device, head_width + 2 * new_width)
    query_heads = (
        arrived[:, :, :head_width]
        .reshape(count_yz, per_device, heads_here, HD)
        .transpose(1, 0, 2, 3)
        .reshape(per_device, kv_heads, count_yz * heads_here // kv_heads, HD)
    )
    key_rows = (
        arrived[:, :, head_width : head_width + new_width]
        .transpose(1, 0, 2)
        .reshape(per_device, kv_heads, HD)
    )
    value_rows = (
        arrived[:, :, head_width + new_width :].transpose(1, 0, 2).reshape(per_device, kv_heads, HD)
    )
    context = attend_slots(query_heads, key_rows, value_rows, cache_keys, cache_values, valid_own)

    outgoing = context.reshape(per_device, count_yz, head_width).transpose(1, 0, 2)
    outgoing = jnp.broadcast_to(outgoing[None], (count_gx,) + outgoing.shape)
    all_columns = lax.all_to_all(
        outgoing.reshape(count_gx * count_yz, per_device, head_width),
        AXES,
        split_axis=0,
        concat_axis=0,
        tiled=True,
    ).reshape(rows, head_width)

    far, near, inner = positions // (RING * block), (positions // block) % RING, positions % block
    row_x = jnp.where(core == 0, x + far, x + near) % RING
    row_y = jnp.where(core == 0, y + near, y + far) % RING
    row_here = (row_x * RING + row_y) * block + inner
    slot_of = jnp.sum(
        jnp.where(row_here[:, None] == positions[None, :], cache_slot[None, :], 0), axis=1
    )
    context_rows = pick(one_hot_rows(slot_of, rows), all_columns)

    def sum_rows(product):
        chunk = RING * block
        parts = {}
        for j in FAR_FIRST:
            part = product(slice(j * chunk, (j + 1) * chunk))
            parts[j] = part if j == 0 else part.astype(BF16)
        total = add_up(parts[0], spread(send_first, parts))
        parts = {k: total[k * block : (k + 1) * block] for k in range(RING)}
        parts = {k: part if k == 0 else part.astype(BF16) for k, part in parts.items()}
        return add_up(parts[0], spread(send_second, parts))

    attended = sum_rows(
        lambda part: jnp.dot(context_rows[part], out_weight, preferred_element_type=F32)
    )
    own_resid = lax.dynamic_slice_in_dim(resid, index_yz * block, block, 0)
    middle = (own_resid.astype(F32) + attended).astype(BF16)
    mid_float = middle.astype(F32)
    scaled = (mid_float * norm_gain[None, :]).astype(BF16)
    high, low = hi_lo(jnp.sum(mid_float * mid_float, axis=1, keepdims=True))
    tail = [jnp.broadcast_to(part, (block, HD // 2)) for part in (high, low)]
    payload = jnp.concatenate([scaled] + tail, axis=1)

    blocks = jnp.concatenate(collect(send_second, payload), axis=0)
    blocks = jnp.concatenate(collect(send_first, blocks), axis=0)

    half = RING * block // CORES
    target = positions[: RING * half] // half
    distance = jnp.zeros_like(target)
    for order_index, j in enumerate(FAR_FIRST):
        distance = jnp.where(target == order_index, j, distance)
    part_x = (z + distance) % RING
    inner_half = positions[: RING * half] % half

    def half_rows(part_core):
        part_y = part_core * (RING // CORES) + inner_half // block
        source = jnp.where(core == 0, part_x * RING + part_y, part_y * RING + part_x)
        matrix = one_hot_rows(source * block + inner_half % block, rows)
        ends = jnp.dot(matrix, blocks[:, width:], preferred_element_type=F32)
        return pick(matrix, blocks[:, :width]), ends[:, : HD // 2] + ends[:, HD // 2 :]

    other_rows, other_squares = half_rows(1 - core)
    own_rows, own_squares = half_rows(core)
    squares = own_squares + send_core(other_squares)
    weights = (gate_weight, up_weight)
    given = [send_core(pick(other_rows, weight)) for weight in weights]
    sums = []
    for weight, gift in zip(weights, given):
        parts = {}
        for pair in range(RING // 2):
            span = slice(pair * 2 * half, (pair + 1) * 2 * half)
            both = jnp.dot(own_rows[span], weight, preferred_element_type=F32)
            both = both + gift[span].astype(F32)
            for i in range(2):
                j = FAR_FIRST[pair * 2 + i]
                part = both[i * half : (i + 1) * half]
                parts[j] = part if j == 0 else part.astype(BF16)
        sums.append(parts)
    square_parts = {j: squares[i * half : (i + 1) * half] for i, j in enumerate(FAR_FIRST)}
    squares = add_up(square_parts[0], spread(send_z, square_parts))
    gate, upper = [add_up(parts[0], spread(send_z, parts)) for parts in sums]
    factor = lax.rsqrt(squares[:, :1] / (width * count_gx) + 1e-05)
    gate = gate * factor
    hidden = (jax.nn.silu(gate) * (upper * factor)).astype(BF16)

    own_hidden = collect(send_z, hidden)
    other_hidden = [send_core(part) for part in own_hidden]
    all_hidden = jnp.concatenate(own_hidden + other_hidden, axis=0)
    place_x = jnp.where(core == 0, far, near)
    place_y = jnp.where(core == 0, near, far)
    place_core = (place_y // (RING // CORES) + core) % CORES
    place_z = (place_x - z) % RING
    place_here = (place_core * RING + place_z) * half + (place_y % (RING // CORES)) * block + inner
    hidden_rows = pick(one_hot_rows(place_here, rows), all_hidden)
    projected = sum_rows(
        lambda part: jnp.dot(hidden_rows[part], down_weight, preferred_element_type=F32)
    )
    return (mid_float + projected).astype(BF16)


def solution(mesh):
    in_specs = (
        P(None, "gx"),
        P(None, "yz"),
        P(None, "yz"),
        P(None, "yz"),
        P(("gx", "yz"), None, None),
        P(("gx", "yz"), None, None),
        P(),
        P(),
        P("yz", "gx"),
        P("gx"),
        P("gx", "yz"),
        P("gx", "yz"),
        P("yz", "gx"),
    )
    out_specs = P("yz", "gx")
    return jax.shard_map(
        on_device, mesh=mesh, in_specs=in_specs, out_specs=out_specs, check_vma=False
    )
```

```python
import functools

import jax
import jax.numpy as jnp
from jax import lax
from jax.experimental import pallas as pl
from jax.experimental.pallas import tpu as pltpu
from jax.sharding import PartitionSpec as P

HD = 128
RING = 4
CORES = 2
AXES = ("gx", "yz")
BF16 = jnp.bfloat16
F32 = jnp.float32
FAR_FIRST = (2, 1, 3, 0)
TURNS = 2


def place(device):
    gx, yz = divmod(device, RING * RING)
    z, core = divmod(gx, CORES)
    x, y = divmod(yz, RING)
    return x, y, z, core


def number(x, y, z, core):
    gx = (z % RING) * CORES + core
    return gx * RING * RING + (x % RING) * RING + y % RING


def pairs(move):
    count = RING * RING * RING * CORES
    return [(d, number(*move(*place(d)))) for d in range(count)]


def send_first(value, step):
    def move(x, y, z, core):
        return (x + step, y, z, core) if core == 0 else (x, y + step, z, core)

    return lax.ppermute(value, AXES, pairs(move))


def send_second(value, step):
    def move(x, y, z, core):
        return (x, y + step, z, core) if core == 0 else (x + step, y, z, core)

    return lax.ppermute(value, AXES, pairs(move))


def send_z(value, step):
    return lax.ppermute(value, AXES, pairs(lambda x, y, z, core: (x, y, z + step, core)))


def send_core(value):
    return lax.ppermute(value, AXES, pairs(lambda x, y, z, core: (x, y, z, 1 - core)))


def spread(send, blocks):
    return [send(blocks[j], j) for j in FAR_FIRST if j != 0]


def collect(send, value):
    got = {0: value}
    for j in (2, 1, 3):
        got[j] = send(value, -j)
    return [got[j] for j in range(RING)]


def add_up(own, others):
    total = own.astype(F32)
    for other in others:
        total = total + other.astype(F32)
    return total


def one_hot_rows(index, count):
    return (index[:, None] == jnp.arange(count, dtype=jnp.int32)[None, :]).astype(BF16)


def pick(matrix, values):
    return jnp.dot(matrix, values, preferred_element_type=F32).astype(BF16)


def local_kernel(body, shapes, *values):
    whole = pl.BlockSpec(memory_space=pltpu.VMEM)
    size = sum(v.size * v.dtype.itemsize for v in values)
    return pl.pallas_call(
        body,
        out_shape=shapes,
        in_specs=[whole] * len(values),
        out_specs=[whole] * len(shapes),
        compiler_params=pltpu.CompilerParams(vmem_limit_bytes=24 * 2**20),
        cost_estimate=pl.CostEstimate(flops=size, bytes_accessed=2 * size, transcendentals=0),
    )(*values)


def ends_of(total):
    high = total.astype(BF16).astype(F32)
    lane = lax.broadcasted_iota(jnp.int32, (total.shape[0], HD), 1)
    return jnp.where(lane < HD // 2, high, total - high).astype(BF16)


def middle_kernel(part, far_one, far_two, far_three, resid, gain, payload, middle):
    chunk, width = part.shape
    piece = chunk // RING
    for k in range(RING):
        here = pl.ds(k * piece, piece)
        total = part[here, :] + resid[here, :].astype(F32)
        for d, other in enumerate((far_one, far_two, far_three)):
            total = total + other[pl.ds((k - d - 1) % RING * piece, piece), :].astype(F32)
        rounded = total.astype(BF16)
        if k == 0:
            middle[...] = rounded
        total = rounded.astype(F32)
        payload[here, :width] = (total * gain[...]).astype(BF16)
        payload[here, width:] = ends_of(jnp.sum(total * total, axis=1, keepdims=True))


def pair_kernel(gate, upper, ends, gate_other, upper_other, ends_other, *payloads):
    half = gate.shape[0] // RING
    width = gate.shape[1]
    for i, payload in enumerate(payloads):
        here = pl.ds(i * half, half)
        payload[:, :width] = (gate[here, :] + gate_other[here, :].astype(F32)).astype(BF16)
        payload[:, width : 2 * width] = (
            upper[here, :] + upper_other[here, :].astype(F32)
        ).astype(BF16)
        both = ends[here, :] + ends_other[here, :]
        payload[:, 2 * width :] = ends_of(both[:, :1] + both[:, HD // 2 : HD // 2 + 1])


def hidden_kernel(model_width, own, one, two, three, hidden):
    width = hidden.shape[1]

    def total(span):
        values = [ref[:, span].astype(F32) for ref in (own, one, two, three)]
        return values[0] + values[1] + values[2] + values[3]

    ends = total(pl.ds(2 * width, HD))
    squares = ends[:, :1] + ends[:, HD // 2 : HD // 2 + 1]
    factor = lax.rsqrt(squares / model_width + 1e-05)
    gate = total(pl.ds(0, width)) * factor
    upper = total(pl.ds(width, width)) * factor
    hidden[...] = (gate / (1.0 + jnp.exp(-gate)) * upper).astype(BF16)


def attend_slots(query_heads, key_rows, value_rows, cache_keys, cache_values, valid):
    slot_count, positions = cache_keys.shape[:2]
    kv_heads, groups = query_heads.shape[1:3]
    scaling = HD ** (-0.5)
    key_heads = cache_keys.reshape(slot_count, positions, kv_heads, HD)
    value_heads = cache_values.reshape(slot_count, positions, kv_heads, HD)
    scores = (
        jnp.einsum("bkgd,bckd->bkgc", query_heads, key_heads, preferred_element_type=F32) * scaling
    )
    new_score = (
        jnp.einsum("bkgd,bkd->bkg", query_heads, key_rows, preferred_element_type=F32) * scaling
    )
    inside = jnp.arange(positions)[None, :] < valid[:, None]
    scores = jnp.where(inside[:, None, None, :], scores, -jnp.inf)
    largest = jnp.maximum(jnp.max(scores, axis=-1), new_score)
    powers = jnp.exp(scores - largest[..., None])
    power_new = jnp.exp(new_score - largest)
    totals = jnp.sum(powers, axis=-1) + power_new
    weights = (powers / totals[..., None]).astype(BF16)
    weight_new = (power_new / totals).astype(BF16)
    context = jnp.einsum("bkgc,bckd->bkgd", weights, value_heads, preferred_element_type=F32)
    context = context + weight_new.astype(F32)[..., None] * value_rows.astype(F32)[:, :, None, :]
    return context.reshape(slot_count, kv_heads * groups * HD).astype(BF16)


def on_device(
    resid,
    queries,
    new_keys,
    new_values,
    cache_keys,
    cache_values,
    lengths,
    cache_slot,
    out_weight,
    norm_gain,
    gate_weight,
    up_weight,
    down_weight,
):
    index_gx = lax.axis_index("gx")
    index_yz = lax.axis_index("yz")
    count_yz = RING * RING
    count_gx = RING * CORES
    z, core = index_gx // CORES, index_gx % CORES
    x, y = index_yz // RING, index_yz % RING
    rows = resid.shape[0]
    width = resid.shape[1]
    per_device = cache_keys.shape[0]
    group_slots = per_device * count_yz
    block = rows // count_yz
    kv_heads = cache_keys.shape[2] // HD
    head_width = out_weight.shape[0]
    heads_here = head_width // HD
    new_width = new_keys.shape[1]

    slot_here = index_gx * group_slots + jnp.arange(group_slots, dtype=jnp.int32)
    routing = cache_slot[None, :] == slot_here[:, None]
    outgoing = pick(
        routing.astype(BF16), jnp.concatenate([queries, new_keys, new_values], axis=1)
    )
    valid = jnp.sum(jnp.where(routing, lengths[None, :], 0), axis=1)
    valid_own = lax.dynamic_slice_in_dim(valid, index_yz * per_device, per_device)
    arrived = lax.all_to_all(outgoing, "yz", split_axis=0, concat_axis=0, tiled=True)
    arrived = arrived.reshape(count_yz, per_device, head_width + 2 * new_width)
    query_heads = (
        arrived[:, :, :head_width]
        .reshape(count_yz, per_device, heads_here, HD)
        .transpose(1, 0, 2, 3)
        .reshape(per_device, kv_heads, count_yz * heads_here // kv_heads, HD)
    )
    key_rows = (
        arrived[:, :, head_width : head_width + new_width]
        .transpose(1, 0, 2)
        .reshape(per_device, kv_heads, HD)
    )
    value_rows = (
        arrived[:, :, head_width + new_width :].transpose(1, 0, 2).reshape(per_device, kv_heads, HD)
    )
    context = attend_slots(query_heads, key_rows, value_rows, cache_keys, cache_values, valid_own)

    outgoing = context.reshape(per_device, count_yz, head_width).transpose(1, 0, 2)
    outgoing = jnp.broadcast_to(outgoing[None], (count_gx,) + outgoing.shape)
    all_columns = lax.all_to_all(
        outgoing.reshape(count_gx * count_yz, per_device, head_width),
        AXES,
        split_axis=0,
        concat_axis=0,
        tiled=True,
    ).reshape(rows, head_width)

    def turn(number):
        positions = jnp.arange(rows // TURNS, dtype=jnp.int32)
        piece = block // TURNS
        chunk = RING * piece

        far, near, inner = positions // chunk, (positions // piece) % RING, positions % piece
        row_x = jnp.where(core == 0, x + far, x + near) % RING
        row_y = jnp.where(core == 0, y + near, y + far) % RING
        row_here = (row_x * RING + row_y) * block + number * piece + inner
        slot_of = jnp.sum(
            jnp.where(row_here[:, None] == jnp.arange(rows)[None, :], cache_slot[None, :], 0), axis=1
        )
        context_rows = pick(one_hot_rows(slot_of, rows), all_columns)

        def sum_first(values, weight):
            parts = {}
            for j in FAR_FIRST:
                part = jnp.dot(
                    values[j * chunk : (j + 1) * chunk], weight, preferred_element_type=F32
                )
                parts[j] = part if j == 0 else part.astype(BF16)
            return add_up(parts[0], spread(send_first, parts))

        part = sum_first(context_rows, out_weight)
        others = collect(send_second, part.astype(BF16))[1:]
        resid_rows = pick(one_hot_rows(row_here[:chunk], rows), resid)
        payload, middle = local_kernel(
            middle_kernel,
            [
                jax.ShapeDtypeStruct((chunk, width + HD), BF16),
                jax.ShapeDtypeStruct((piece, width), BF16),
            ],
            part,
            *others,
            resid_rows,
            norm_gain[None, :],
        )
        blocks = jnp.concatenate(collect(send_first, payload), axis=0)

        half = chunk // CORES
        target = positions[: RING * half] // half
        distance = jnp.zeros_like(target)
        for order_index, j in enumerate(FAR_FIRST):
            distance = jnp.where(target == order_index, j, distance)
        part_x = (z + distance) % RING
        inner_half = positions[: RING * half] % half

        def half_rows(part_core):
            part_y = part_core * (RING // CORES) + inner_half // piece
            source = jnp.where(core == 0, part_x * RING + part_y, part_y * RING + part_x)
            matrix = one_hot_rows(source * piece + inner_half % piece, rows // TURNS)
            ends = jnp.dot(matrix, blocks[:, width:], preferred_element_type=F32)
            return pick(matrix, blocks[:, :width]), ends

        other_rows, other_ends = half_rows(1 - core)
        own_rows, own_ends = half_rows(core)
        other_ends = send_core(other_ends)
        other_gate = send_core(pick(other_rows, gate_weight))
        other_upper = send_core(pick(other_rows, up_weight))
        hidden_width = gate_weight.shape[1]
        payloads = local_kernel(
            pair_kernel,
            [jax.ShapeDtypeStruct((half, 2 * hidden_width + HD), BF16)] * RING,
            jnp.dot(own_rows, gate_weight, preferred_element_type=F32),
            jnp.dot(own_rows, up_weight, preferred_element_type=F32),
            own_ends,
            other_gate,
            other_upper,
            other_ends,
        )
        parts = dict(zip(FAR_FIRST, payloads))
        (hidden,) = local_kernel(
            functools.partial(hidden_kernel, width * count_gx),
            [jax.ShapeDtypeStruct((half, hidden_width), BF16)],
            parts[0],
            *spread(send_z, parts),
        )

        own_hidden = jnp.concatenate(collect(send_z, hidden), axis=0)
        all_hidden = jnp.concatenate([own_hidden, send_core(own_hidden)], axis=0)
        place_x = jnp.where(core == 0, far, near)
        place_y = jnp.where(core == 0, near, far)
        place_core = (place_y // (RING // CORES) + core) % CORES
        place_z = (place_x - z) % RING
        place_here = (
            (place_core * RING + place_z) * half + (place_y % (RING // CORES)) * piece + inner
        )
        hidden_rows = pick(one_hot_rows(place_here, rows // TURNS), all_hidden)
        part = sum_first(hidden_rows, down_weight)
        parts = {k: part[k * piece : (k + 1) * piece] for k in range(RING)}
        parts = {k: part if k == 0 else part.astype(BF16) for k, part in parts.items()}
        projected = add_up(parts[0], spread(send_second, parts))
        return (middle.astype(F32) + projected).astype(BF16)

    return jnp.concatenate([turn(number) for number in range(TURNS)], axis=0)


def solution(mesh):
    in_specs = (
        P(None, "gx"),
        P(None, "yz"),
        P(None, "yz"),
        P(None, "yz"),
        P(("gx", "yz"), None, None),
        P(("gx", "yz"), None, None),
        P(),
        P(),
        P("yz", "gx"),
        P("gx"),
        P("gx", "yz"),
        P("gx", "yz"),
        P("yz", "gx"),
    )
    out_specs = P("yz", "gx")
    return jax.shard_map(
        on_device, mesh=mesh, in_specs=in_specs, out_specs=out_specs, check_vma=False
    )
```

```python
import functools

import jax
import jax.numpy as jnp
from jax import lax
from jax.experimental import pallas as pl
from jax.experimental.pallas import tpu as pltpu
from jax.sharding import PartitionSpec as P

HD = 128
RING = 4
CORES = 2
AXES = ("gx", "yz")
BF16 = jnp.bfloat16
F32 = jnp.float32
FAR_FIRST = (2, 1, 3, 0)
TURNS = 2


def place(device):
    gx, yz = divmod(device, RING * RING)
    z, core = divmod(gx, CORES)
    x, y = divmod(yz, RING)
    return x, y, z, core


def number(x, y, z, core):
    gx = (z % RING) * CORES + core
    return gx * RING * RING + (x % RING) * RING + y % RING


def pairs(move):
    count = RING * RING * RING * CORES
    return [(d, number(*move(*place(d)))) for d in range(count)]


def send_first(value, step):
    def move(x, y, z, core):
        return (x + step, y, z, core) if core == 0 else (x, y + step, z, core)

    return lax.ppermute(value, AXES, pairs(move))


def send_second(value, step):
    def move(x, y, z, core):
        return (x, y + step, z, core) if core == 0 else (x + step, y, z, core)

    return lax.ppermute(value, AXES, pairs(move))


def send_z(value, step):
    return lax.ppermute(value, AXES, pairs(lambda x, y, z, core: (x, y, z + step, core)))


def send_core(value):
    return lax.ppermute(value, AXES, pairs(lambda x, y, z, core: (x, y, z, 1 - core)))


def spread(send, blocks):
    return [send(blocks[j], j) for j in FAR_FIRST if j != 0]


def collect(send, value):
    got = {0: value}
    for j in (2, 1, 3):
        got[j] = send(value, -j)
    return [got[j] for j in range(RING)]


def add_up(own, others):
    total = own.astype(F32)
    for other in others:
        total = total + other.astype(F32)
    return total


def one_hot_rows(index, count):
    return (index[:, None] == jnp.arange(count, dtype=jnp.int32)[None, :]).astype(BF16)


def after(value, earlier):
    return lax.optimization_barrier((value, earlier))[0]


def pick(matrix, values):
    return jnp.dot(matrix, values, preferred_element_type=F32).astype(BF16)


def local_kernel(body, shapes, *values):
    whole = pl.BlockSpec(memory_space=pltpu.VMEM)
    size = sum(v.size * v.dtype.itemsize for v in values)
    return pl.pallas_call(
        body,
        out_shape=shapes,
        in_specs=[whole] * len(values),
        out_specs=[whole] * len(shapes),
        compiler_params=pltpu.CompilerParams(vmem_limit_bytes=24 * 2**20),
        cost_estimate=pl.CostEstimate(flops=size, bytes_accessed=2 * size, transcendentals=0),
    )(*values)


def ends_of(total):
    high = total.astype(BF16).astype(F32)
    lane = lax.broadcasted_iota(jnp.int32, (total.shape[0], HD), 1)
    return jnp.where(lane < HD // 2, high, total - high).astype(BF16)


def middle_kernel(part, far_one, far_two, far_three, resid, gain, payload, middle):
    chunk, width = part.shape
    piece = chunk // RING
    for k in range(RING):
        here = pl.ds(k * piece, piece)
        total = part[here, :] + resid[here, :].astype(F32)
        for d, other in enumerate((far_one, far_two, far_three)):
            total = total + other[pl.ds((k - d - 1) % RING * piece, piece), :].astype(F32)
        rounded = total.astype(BF16)
        if k == 0:
            middle[...] = rounded
        total = rounded.astype(F32)
        payload[here, :width] = (total * gain[...]).astype(BF16)
        payload[here, width:] = ends_of(jnp.sum(total * total, axis=1, keepdims=True))


def gift_kernel(gate, upper, ends, gift):
    width = gate.shape[1]
    gift[:, :width] = gate[...]
    gift[:, width : 2 * width] = upper[...]
    gift[:, 2 * width :] = ends[...]


def pair_kernel(gate, upper, ends, other, *payloads):
    half = gate.shape[0] // RING
    width = gate.shape[1]
    for i, payload in enumerate(payloads):
        here = pl.ds(i * half, half)
        payload[:, :width] = (gate[here, :] + other[here, :width].astype(F32)).astype(BF16)
        payload[:, width : 2 * width] = (
            upper[here, :] + other[here, width : 2 * width].astype(F32)
        ).astype(BF16)
        both = ends[here, :].astype(F32) + other[here, 2 * width :].astype(F32)
        payload[:, 2 * width :] = ends_of(both[:, :1] + both[:, HD // 2 : HD // 2 + 1])


def hidden_kernel(model_width, own, one, two, three, hidden):
    width = hidden.shape[1]

    def total(span):
        values = [ref[:, span].astype(F32) for ref in (own, one, two, three)]
        return values[0] + values[1] + values[2] + values[3]

    ends = total(pl.ds(2 * width, HD))
    squares = ends[:, :1] + ends[:, HD // 2 : HD // 2 + 1]
    factor = lax.rsqrt(squares / model_width + 1e-05)
    gate = total(pl.ds(0, width)) * factor
    upper = total(pl.ds(width, width)) * factor
    hidden[...] = (gate / (1.0 + jnp.exp(-gate)) * upper).astype(BF16)


def attend_slots(query_heads, key_rows, value_rows, cache_keys, cache_values, valid):
    slot_count, positions = cache_keys.shape[:2]
    kv_heads, groups = query_heads.shape[1:3]
    scaling = HD ** (-0.5)
    key_heads = cache_keys.reshape(slot_count, positions, kv_heads, HD)
    value_heads = cache_values.reshape(slot_count, positions, kv_heads, HD)
    scores = (
        jnp.einsum("bkgd,bckd->bkgc", query_heads, key_heads, preferred_element_type=F32) * scaling
    )
    new_score = (
        jnp.einsum("bkgd,bkd->bkg", query_heads, key_rows, preferred_element_type=F32) * scaling
    )
    inside = jnp.arange(positions)[None, :] < valid[:, None]
    scores = jnp.where(inside[:, None, None, :], scores, -jnp.inf)
    largest = jnp.maximum(jnp.max(scores, axis=-1), new_score)
    powers = jnp.exp(scores - largest[..., None])
    power_new = jnp.exp(new_score - largest)
    totals = jnp.sum(powers, axis=-1) + power_new
    weights = (powers / totals[..., None]).astype(BF16)
    weight_new = (power_new / totals).astype(BF16)
    context = jnp.einsum("bkgc,bckd->bkgd", weights, value_heads, preferred_element_type=F32)
    context = context + weight_new.astype(F32)[..., None] * value_rows.astype(F32)[:, :, None, :]
    return context.reshape(slot_count, kv_heads * groups * HD).astype(BF16)


def on_device(
    resid,
    queries,
    new_keys,
    new_values,
    cache_keys,
    cache_values,
    lengths,
    cache_slot,
    out_weight,
    norm_gain,
    gate_weight,
    up_weight,
    down_weight,
):
    index_gx = lax.axis_index("gx")
    index_yz = lax.axis_index("yz")
    count_yz = RING * RING
    count_gx = RING * CORES
    z, core = index_gx // CORES, index_gx % CORES
    x, y = index_yz // RING, index_yz % RING
    rows = resid.shape[0]
    width = resid.shape[1]
    per_device = cache_keys.shape[0]
    group_slots = per_device * count_yz
    block = rows // count_yz
    kv_heads = cache_keys.shape[2] // HD
    head_width = out_weight.shape[0]
    heads_here = head_width // HD
    new_width = new_keys.shape[1]

    slot_here = index_gx * group_slots + jnp.arange(group_slots, dtype=jnp.int32)
    routing = cache_slot[None, :] == slot_here[:, None]
    outgoing = jnp.concatenate(
        [pick(routing.astype(BF16), values) for values in (queries, new_keys, new_values)], axis=1
    )
    valid = jnp.sum(jnp.where(routing, lengths[None, :], 0), axis=1)
    valid_own = lax.dynamic_slice_in_dim(valid, index_yz * per_device, per_device)
    arrived = lax.all_to_all(outgoing, "yz", split_axis=0, concat_axis=0, tiled=True)
    arrived = arrived.reshape(count_yz, per_device, head_width + 2 * new_width)
    query_heads = (
        arrived[:, :, :head_width]
        .reshape(count_yz, per_device, heads_here, HD)
        .transpose(1, 0, 2, 3)
        .reshape(per_device, kv_heads, count_yz * heads_here // kv_heads, HD)
    )
    key_rows = (
        arrived[:, :, head_width : head_width + new_width]
        .transpose(1, 0, 2)
        .reshape(per_device, kv_heads, HD)
    )
    value_rows = (
        arrived[:, :, head_width + new_width :].transpose(1, 0, 2).reshape(per_device, kv_heads, HD)
    )
    context = attend_slots(query_heads, key_rows, value_rows, cache_keys, cache_values, valid_own)

    outgoing = context.reshape(per_device, count_yz, head_width).transpose(1, 0, 2)
    outgoing = jnp.broadcast_to(outgoing[None], (count_gx,) + outgoing.shape)
    all_columns = lax.all_to_all(
        outgoing.reshape(count_gx * count_yz, per_device, head_width),
        AXES,
        split_axis=0,
        concat_axis=0,
        tiled=True,
    ).reshape(rows, head_width)

    positions = jnp.arange(rows // TURNS, dtype=jnp.int32)
    piece = block // TURNS
    chunk = RING * piece
    half = chunk // CORES
    hidden_width = gate_weight.shape[1]
    far, near, inner = positions // chunk, (positions // piece) % RING, positions % piece

    def sum_first(values, weight):
        parts = {}
        for j in FAR_FIRST:
            part = jnp.dot(values[j * chunk : (j + 1) * chunk], weight, preferred_element_type=F32)
            parts[j] = part if j == 0 else part.astype(BF16)
        return add_up(parts[0], spread(send_first, parts))

    def project(number):
        row_x = jnp.where(core == 0, x + far, x + near) % RING
        row_y = jnp.where(core == 0, y + near, y + far) % RING
        row_here = (row_x * RING + row_y) * block + number * piece + inner
        slot_of = jnp.sum(
            jnp.where(row_here[:, None] == jnp.arange(rows)[None, :], cache_slot[None, :], 0), axis=1
        )
        context_rows = pick(one_hot_rows(slot_of, rows), all_columns)
        part = sum_first(context_rows, out_weight)
        others = collect(send_second, part.astype(BF16))[1:]
        resid_rows = pick(one_hot_rows(row_here[:chunk], rows), resid)
        payload, middle = local_kernel(
            middle_kernel,
            [
                jax.ShapeDtypeStruct((chunk, width + HD), BF16),
                jax.ShapeDtypeStruct((piece, width), BF16),
            ],
            part,
            *others,
            resid_rows,
            norm_gain[None, :],
        )
        return middle, jnp.concatenate(collect(send_first, payload), axis=0)

    def gate_and_up(blocks):
        target = positions[: RING * half] // half
        distance = jnp.zeros_like(target)
        for order_index, j in enumerate(FAR_FIRST):
            distance = jnp.where(target == order_index, j, distance)
        part_x = (z + distance) % RING
        inner_half = positions[: RING * half] % half

        def half_rows(part_core):
            part_y = part_core * (RING // CORES) + inner_half // piece
            source = jnp.where(core == 0, part_x * RING + part_y, part_y * RING + part_x)
            matrix = one_hot_rows(source * piece + inner_half % piece, rows // TURNS)
            return pick(matrix, blocks[:, :width]), pick(matrix, blocks[:, width:])

        other_rows, other_ends = half_rows(1 - core)
        own_rows, own_ends = half_rows(core)
        sums_width = 2 * hidden_width + HD
        (gift,) = local_kernel(
            gift_kernel,
            [jax.ShapeDtypeStruct((RING * half, sums_width), BF16)],
            pick(other_rows, gate_weight),
            pick(other_rows, up_weight),
            other_ends,
        )
        payloads = local_kernel(
            pair_kernel,
            [jax.ShapeDtypeStruct((half, sums_width), BF16)] * RING,
            jnp.dot(own_rows, gate_weight, preferred_element_type=F32),
            jnp.dot(own_rows, up_weight, preferred_element_type=F32),
            own_ends,
            send_core(gift),
        )
        return dict(zip(FAR_FIRST, payloads))

    def activate(own, others):
        (hidden,) = local_kernel(
            functools.partial(hidden_kernel, width * count_gx),
            [jax.ShapeDtypeStruct((half, hidden_width), BF16)],
            own,
            *others,
        )
        own_hidden = jnp.concatenate(collect(send_z, hidden), axis=0)
        return hidden, jnp.concatenate([own_hidden, send_core(own_hidden)], axis=0)

    def finish(middle, all_hidden):
        place_x = jnp.where(core == 0, far, near)
        place_y = jnp.where(core == 0, near, far)
        place_core = (place_y // (RING // CORES) + core) % CORES
        place_z = (place_x - z) % RING
        place_here = (
            (place_core * RING + place_z) * half + (place_y % (RING // CORES)) * piece + inner
        )
        hidden_rows = pick(one_hot_rows(place_here, rows // TURNS), all_hidden)
        part = sum_first(hidden_rows, down_weight)
        parts = {k: part[k * piece : (k + 1) * piece] for k in range(RING)}
        parts = {k: part if k == 0 else part.astype(BF16) for k, part in parts.items()}
        projected = add_up(parts[0], spread(send_second, parts))
        return (middle.astype(F32) + projected).astype(BF16)

    middles, blocks = zip(*[project(number) for number in range(TURNS)])
    parts = [gate_and_up(blocks[0])]
    for number in range(1, TURNS):
        parts.append(gate_and_up(blocks[number]))
    results = []
    for number in range(TURNS):
        own = parts[number][0]
        hidden, all_hidden = activate(own, spread(send_z, parts[number]))
        results.append(finish(middles[number], all_hidden))
    return jnp.concatenate(results, axis=0)


def solution(mesh):
    in_specs = (
        P(None, "gx"),
        P(None, "yz"),
        P(None, "yz"),
        P(None, "yz"),
        P(("gx", "yz"), None, None),
        P(("gx", "yz"), None, None),
        P(),
        P(),
        P("yz", "gx"),
        P("gx"),
        P("gx", "yz"),
        P("gx", "yz"),
        P("yz", "gx"),
    )
    out_specs = P("yz", "gx")
    return jax.shard_map(
        on_device, mesh=mesh, in_specs=in_specs, out_specs=out_specs, check_vma=False
    )
```

```python
import functools

import jax
import jax.numpy as jnp
from jax import lax
from jax.experimental import pallas as pl
from jax.experimental.pallas import tpu as pltpu
from jax.sharding import PartitionSpec as P

HD = 128
RING = 4
CORES = 2
AXES = ("gx", "yz")
BF16 = jnp.bfloat16
F32 = jnp.float32
FAR_FIRST = (2, 1, 3, 0)
TURNS = 2


def place(device):
    gx, yz = divmod(device, RING * RING)
    z, core = divmod(gx, CORES)
    x, y = divmod(yz, RING)
    return x, y, z, core


def number(x, y, z, core):
    gx = (z % RING) * CORES + core
    return gx * RING * RING + (x % RING) * RING + y % RING


def pairs(move):
    count = RING * RING * RING * CORES
    return [(d, number(*move(*place(d)))) for d in range(count)]


def send_first(value, step):
    def move(x, y, z, core):
        return (x + step, y, z, core) if core == 0 else (x, y + step, z, core)

    return lax.ppermute(value, AXES, pairs(move))


def send_second(value, step):
    def move(x, y, z, core):
        return (x, y + step, z, core) if core == 0 else (x + step, y, z, core)

    return lax.ppermute(value, AXES, pairs(move))


def send_z(value, step):
    return lax.ppermute(value, AXES, pairs(lambda x, y, z, core: (x, y, z + step, core)))


def send_core(value):
    return lax.ppermute(value, AXES, pairs(lambda x, y, z, core: (x, y, z, 1 - core)))


def spread(send, blocks):
    return [send(blocks[j], j) for j in FAR_FIRST if j != 0]


def collect(send, value):
    got = {0: value}
    for j in (2, 1, 3):
        got[j] = send(value, -j)
    return [got[j] for j in range(RING)]


def add_up(own, others):
    total = own.astype(F32)
    for other in others:
        total = total + other.astype(F32)
    return total


def one_hot_rows(index, count):
    return (index[:, None] == jnp.arange(count, dtype=jnp.int32)[None, :]).astype(BF16)


def after(value, earlier):
    return lax.optimization_barrier((value, earlier))[0]


def pick(matrix, values):
    return jnp.dot(matrix, values, preferred_element_type=F32).astype(BF16)


def local_kernel(body, shapes, *values):
    whole = pl.BlockSpec(memory_space=pltpu.VMEM)
    size = sum(v.size * v.dtype.itemsize for v in values)
    return pl.pallas_call(
        body,
        out_shape=shapes,
        in_specs=[whole] * len(values),
        out_specs=[whole] * len(shapes),
        compiler_params=pltpu.CompilerParams(vmem_limit_bytes=24 * 2**20),
        cost_estimate=pl.CostEstimate(flops=size, bytes_accessed=2 * size, transcendentals=0),
    )(*values)


def ends_of(total):
    high = total.astype(BF16).astype(F32)
    lane = lax.broadcasted_iota(jnp.int32, (total.shape[0], HD), 1)
    return jnp.where(lane < HD // 2, high, total - high).astype(BF16)


def middle_kernel(part, far_one, far_two, far_three, resid, gain, payload, middle):
    chunk, width = part.shape
    piece = chunk // RING
    for k in range(RING):
        here = pl.ds(k * piece, piece)
        total = part[here, :] + resid[here, :].astype(F32)
        for d, other in enumerate((far_one, far_two, far_three)):
            total = total + other[pl.ds((k - d - 1) % RING * piece, piece), :].astype(F32)
        rounded = total.astype(BF16)
        if k == 0:
            middle[...] = rounded
        total = rounded.astype(F32)
        payload[here, :width] = (total * gain[...]).astype(BF16)
        payload[here, width:] = ends_of(jnp.sum(total * total, axis=1, keepdims=True))


def gift_kernel(gate, upper, ends, gift):
    width = gate.shape[1]
    here = pl.ds(0, gift.shape[0])
    gift[:, :width] = gate[here, :]
    gift[:, width : 2 * width] = upper[here, :]
    gift[:, 2 * width :] = ends[here, :]


def pair_kernel(gate, upper, ends, other, *payloads):
    half = other.shape[0] // RING
    width = gate.shape[1]
    for i, payload in enumerate(payloads):
        here, there = pl.ds((RING + i) * half, half), pl.ds(i * half, half)
        for k, ref in enumerate((gate, upper)):
            span = pl.ds(k * width, width)
            payload[:, span] = (
                ref[here, :].astype(F32) + other[there, span].astype(F32)
            ).astype(BF16)
        both = ends[here, :].astype(F32) + other[there, 2 * width :].astype(F32)
        payload[:, 2 * width :] = ends_of(both[:, :1] + both[:, HD // 2 : HD // 2 + 1])


def hidden_kernel(model_width, own, one, two, three, hidden):
    width = hidden.shape[1]

    def total(span):
        values = [ref[:, span].astype(F32) for ref in (own, one, two, three)]
        return values[0] + values[1] + values[2] + values[3]

    ends = total(pl.ds(2 * width, HD))
    squares = ends[:, :1] + ends[:, HD // 2 : HD // 2 + 1]
    factor = lax.rsqrt(squares / model_width + 1e-05)
    gate = total(pl.ds(0, width)) * factor
    upper = total(pl.ds(width, width)) * factor
    hidden[...] = (gate / (1.0 + jnp.exp(-gate)) * upper).astype(BF16)


def attend_slots(query_heads, key_rows, value_rows, cache_keys, cache_values, valid):
    slot_count, positions = cache_keys.shape[:2]
    kv_heads, groups = query_heads.shape[1:3]
    scaling = HD ** (-0.5)
    key_heads = cache_keys.reshape(slot_count, positions, kv_heads, HD)
    value_heads = cache_values.reshape(slot_count, positions, kv_heads, HD)
    scores = (
        jnp.einsum("bkgd,bckd->bkgc", query_heads, key_heads, preferred_element_type=F32) * scaling
    )
    new_score = (
        jnp.einsum("bkgd,bkd->bkg", query_heads, key_rows, preferred_element_type=F32) * scaling
    )
    inside = jnp.arange(positions)[None, :] < valid[:, None]
    scores = jnp.where(inside[:, None, None, :], scores, -jnp.inf)
    largest = jnp.maximum(jnp.max(scores, axis=-1), new_score)
    powers = jnp.exp(scores - largest[..., None])
    power_new = jnp.exp(new_score - largest)
    totals = jnp.sum(powers, axis=-1) + power_new
    weights = (powers / totals[..., None]).astype(BF16)
    weight_new = (power_new / totals).astype(BF16)
    context = jnp.einsum("bkgc,bckd->bkgd", weights, value_heads, preferred_element_type=F32)
    context = context + weight_new.astype(F32)[..., None] * value_rows.astype(F32)[:, :, None, :]
    return context.reshape(slot_count, kv_heads * groups * HD).astype(BF16)


def on_device(
    resid,
    queries,
    new_keys,
    new_values,
    cache_keys,
    cache_values,
    lengths,
    cache_slot,
    out_weight,
    norm_gain,
    gate_weight,
    up_weight,
    down_weight,
):
    index_gx = lax.axis_index("gx")
    index_yz = lax.axis_index("yz")
    count_yz = RING * RING
    count_gx = RING * CORES
    z, core = index_gx // CORES, index_gx % CORES
    x, y = index_yz // RING, index_yz % RING
    rows = resid.shape[0]
    width = resid.shape[1]
    per_device = cache_keys.shape[0]
    group_slots = per_device * count_yz
    block = rows // count_yz
    kv_heads = cache_keys.shape[2] // HD
    head_width = out_weight.shape[0]
    heads_here = head_width // HD
    new_width = new_keys.shape[1]

    slot_here = index_gx * group_slots + jnp.arange(group_slots, dtype=jnp.int32)
    routing = cache_slot[None, :] == slot_here[:, None]
    outgoing = jnp.concatenate(
        [pick(routing.astype(BF16), values) for values in (queries, new_keys, new_values)], axis=1
    )
    valid = jnp.sum(jnp.where(routing, lengths[None, :], 0), axis=1)
    valid_own = lax.dynamic_slice_in_dim(valid, index_yz * per_device, per_device)
    arrived = lax.all_to_all(outgoing, "yz", split_axis=0, concat_axis=0, tiled=True)
    arrived = arrived.reshape(count_yz, per_device, head_width + 2 * new_width)
    query_heads = (
        arrived[:, :, :head_width]
        .reshape(count_yz, per_device, heads_here, HD)
        .transpose(1, 0, 2, 3)
        .reshape(per_device, kv_heads, count_yz * heads_here // kv_heads, HD)
    )
    key_rows = (
        arrived[:, :, head_width : head_width + new_width]
        .transpose(1, 0, 2)
        .reshape(per_device, kv_heads, HD)
    )
    value_rows = (
        arrived[:, :, head_width + new_width :].transpose(1, 0, 2).reshape(per_device, kv_heads, HD)
    )
    context = attend_slots(query_heads, key_rows, value_rows, cache_keys, cache_values, valid_own)

    outgoing = context.reshape(per_device, count_yz, head_width).transpose(1, 0, 2)
    outgoing = jnp.broadcast_to(outgoing[None], (count_gx,) + outgoing.shape)
    all_columns = lax.all_to_all(
        outgoing.reshape(count_gx * count_yz, per_device, head_width),
        AXES,
        split_axis=0,
        concat_axis=0,
        tiled=True,
    ).reshape(rows, head_width)

    positions = jnp.arange(rows // TURNS, dtype=jnp.int32)
    piece = block // TURNS
    chunk = RING * piece
    half = chunk // CORES
    hidden_width = gate_weight.shape[1]
    far, near, inner = positions // chunk, (positions // piece) % RING, positions % piece

    def sum_first(values, weight):
        total = pick(values, weight)
        parts = {j: total[j * chunk : (j + 1) * chunk] for j in range(RING)}
        return add_up(parts[0], spread(send_first, parts))

    def rows_here(number):
        row_x = jnp.where(core == 0, x + far, x + near) % RING
        row_y = jnp.where(core == 0, y + near, y + far) % RING
        return (row_x * RING + row_y) * block + number * piece + inner

    every_row = jnp.concatenate([rows_here(number) for number in range(TURNS)])
    slot_of = jnp.sum(
        jnp.where(every_row[:, None] == jnp.arange(rows)[None, :], cache_slot[None, :], 0), axis=1
    )
    every_context = pick(one_hot_rows(slot_of, rows), all_columns)
    first_rows = jnp.concatenate([rows_here(number)[:chunk] for number in range(TURNS)])
    every_resid = pick(one_hot_rows(first_rows, rows), resid)

    def project(number):
        context_rows = every_context[number * RING * chunk : (number + 1) * RING * chunk]
        resid_rows = every_resid[number * chunk : (number + 1) * chunk]
        part = sum_first(context_rows, out_weight)
        others = collect(send_second, part.astype(BF16))[1:]
        payload, middle = local_kernel(
            middle_kernel,
            [
                jax.ShapeDtypeStruct((chunk, width + HD), BF16),
                jax.ShapeDtypeStruct((piece, width), BF16),
            ],
            part,
            *others,
            resid_rows,
            norm_gain[None, :],
        )
        return middle, jnp.concatenate(collect(send_first, payload), axis=0)

    def gate_and_up(blocks):
        target = positions[: RING * half] // half
        distance = jnp.zeros_like(target)
        for order_index, j in enumerate(FAR_FIRST):
            distance = jnp.where(target == order_index, j, distance)
        part_x = (z + distance) % RING
        inner_half = positions[: RING * half] % half

        def half_rows(part_core):
            part_y = part_core * (RING // CORES) + inner_half // piece
            source = jnp.where(core == 0, part_x * RING + part_y, part_y * RING + part_x)
            return source * piece + inner_half % piece

        source = jnp.concatenate([half_rows(1 - core), half_rows(core)])
        sorted_rows = pick(one_hot_rows(source, rows // TURNS), blocks)
        gate = pick(sorted_rows[:, :width], gate_weight)
        upper = pick(sorted_rows[:, :width], up_weight)
        ends = sorted_rows[:, width:]
        sums_width = 2 * hidden_width + HD
        (gift,) = local_kernel(
            gift_kernel,
            [jax.ShapeDtypeStruct((RING * half, sums_width), BF16)],
            gate,
            upper,
            ends,
        )
        payloads = local_kernel(
            pair_kernel,
            [jax.ShapeDtypeStruct((half, sums_width), BF16)] * RING,
            gate,
            upper,
            ends,
            send_core(gift),
        )
        return dict(zip(FAR_FIRST, payloads))

    def activate(own, others):
        (hidden,) = local_kernel(
            functools.partial(hidden_kernel, width * count_gx),
            [jax.ShapeDtypeStruct((half, hidden_width), BF16)],
            own,
            *others,
        )
        own_hidden = jnp.concatenate(collect(send_z, hidden), axis=0)
        return hidden, jnp.concatenate([own_hidden, send_core(own_hidden)], axis=0)

    def finish(middle, all_hidden):
        place_x = jnp.where(core == 0, far, near)
        place_y = jnp.where(core == 0, near, far)
        place_core = (place_y // (RING // CORES) + core) % CORES
        place_z = (place_x - z) % RING
        place_here = (
            (place_core * RING + place_z) * half + (place_y % (RING // CORES)) * piece + inner
        )
        hidden_rows = pick(one_hot_rows(place_here, rows // TURNS), all_hidden)
        part = sum_first(hidden_rows, down_weight)
        parts = {k: part[k * piece : (k + 1) * piece] for k in range(RING)}
        parts = {k: part if k == 0 else part.astype(BF16) for k, part in parts.items()}
        projected = add_up(parts[0], spread(send_second, parts))
        return (middle.astype(F32) + projected).astype(BF16)

    middles, blocks = zip(*[project(number) for number in range(TURNS)])
    parts = [gate_and_up(blocks[0])]
    for number in range(1, TURNS):
        parts.append(gate_and_up(blocks[number]))
    results = []
    for number in range(TURNS):
        own = parts[number][0]
        hidden, all_hidden = activate(own, spread(send_z, parts[number]))
        results.append(finish(middles[number], all_hidden))
    return jnp.concatenate(results, axis=0)


def solution(mesh):
    in_specs = (
        P(None, "gx"),
        P(None, "yz"),
        P(None, "yz"),
        P(None, "yz"),
        P(("gx", "yz"), None, None),
        P(("gx", "yz"), None, None),
        P(),
        P(),
        P("yz", "gx"),
        P("gx"),
        P("gx", "yz"),
        P("gx", "yz"),
        P("yz", "gx"),
    )
    out_specs = P("yz", "gx")
    return jax.shard_map(
        on_device, mesh=mesh, in_specs=in_specs, out_specs=out_specs, check_vma=False
    )
```

```python
import functools

import jax
import jax.numpy as jnp
from jax import lax
from jax.experimental import pallas as pl
from jax.experimental.pallas import tpu as pltpu
from jax.sharding import PartitionSpec as P

HD = 128
RING = 4
CORES = 2
AXES = ("gx", "yz")
BF16 = jnp.bfloat16
F32 = jnp.float32
FAR_FIRST = (2, 1, 3, 0)
TURNS = 2


def place(device):
    gx, yz = divmod(device, RING * RING)
    z, core = divmod(gx, CORES)
    x, y = divmod(yz, RING)
    return x, y, z, core


def number(x, y, z, core):
    gx = (z % RING) * CORES + core
    return gx * RING * RING + (x % RING) * RING + y % RING


def pairs(move):
    count = RING * RING * RING * CORES
    return [(d, number(*move(*place(d)))) for d in range(count)]


def send_first(value, step):
    def move(x, y, z, core):
        return (x + step, y, z, core) if core == 0 else (x, y + step, z, core)

    return lax.ppermute(value, AXES, pairs(move))


def send_second(value, step):
    def move(x, y, z, core):
        return (x, y + step, z, core) if core == 0 else (x + step, y, z, core)

    return lax.ppermute(value, AXES, pairs(move))


def send_z(value, step):
    return lax.ppermute(value, AXES, pairs(lambda x, y, z, core: (x, y, z + step, core)))


def send_core(value):
    return lax.ppermute(value, AXES, pairs(lambda x, y, z, core: (x, y, z, 1 - core)))


def spread(send, blocks):
    return [send(blocks[j], j) for j in FAR_FIRST if j != 0]


def collect(send, value):
    got = {0: value}
    for j in (2, 1, 3):
        got[j] = send(value, -j)
    return [got[j] for j in range(RING)]


def add_up(own, others):
    total = own.astype(F32)
    for other in others:
        total = total + other.astype(F32)
    return total


def one_hot_rows(index, count):
    return (index[:, None] == jnp.arange(count, dtype=jnp.int32)[None, :]).astype(BF16)


def after(value, earlier):
    return lax.optimization_barrier((value, earlier))[0]


def pick(matrix, values):
    return jnp.dot(matrix, values, preferred_element_type=F32).astype(BF16)


def local_kernel(body, shapes, *values):
    whole = pl.BlockSpec(memory_space=pltpu.VMEM)
    size = sum(v.size * v.dtype.itemsize for v in values)
    return pl.pallas_call(
        body,
        out_shape=shapes,
        in_specs=[whole] * len(values),
        out_specs=[whole] * len(shapes),
        compiler_params=pltpu.CompilerParams(vmem_limit_bytes=24 * 2**20),
        cost_estimate=pl.CostEstimate(flops=size, bytes_accessed=2 * size, transcendentals=0),
    )(*values)


def ends_of(total):
    high = total.astype(BF16).astype(F32)
    lane = lax.broadcasted_iota(jnp.int32, (total.shape[0], HD), 1)
    return jnp.where(lane < HD // 2, high, total - high).astype(BF16)


def middle_kernel(part, far_one, far_two, far_three, resid, gain, payload, middle):
    chunk, width = part.shape
    piece = chunk // RING

    @pl.loop(0, RING)
    def _(k):
        here = pl.ds(pl.multiple_of(k * piece, piece), piece)
        total = part[here, :] + resid[here, :].astype(F32)
        for d, other in enumerate((far_one, far_two, far_three)):
            start = pl.multiple_of(lax.rem(k + RING - d - 1, RING) * piece, piece)
            total = total + other[pl.ds(start, piece), :].astype(F32)
        rounded = total.astype(BF16)

        @pl.when(k == 0)
        def _():
            middle[...] = rounded

        total = rounded.astype(F32)
        payload[here, :width] = (total * gain[...]).astype(BF16)
        payload[here, width:] = ends_of(jnp.sum(total * total, axis=1, keepdims=True))


def gift_kernel(gate, upper, ends, gift):
    width = gate.shape[1]
    here = pl.ds(0, gift.shape[0])
    gift[:, :width] = gate[here, :]
    gift[:, width : 2 * width] = upper[here, :]
    gift[:, 2 * width :] = ends[here, :]


def pair_kernel(gate, upper, ends, other, *payloads):
    half = other.shape[0] // RING
    width = gate.shape[1]
    for i, payload in enumerate(payloads):
        here, there = pl.ds((RING + i) * half, half), pl.ds(i * half, half)
        for k, ref in enumerate((gate, upper)):

            @pl.loop(0, width // (2 * HD))
            def _(step):
                start = pl.multiple_of(step * 2 * HD, 2 * HD)
                span = pl.ds(k * width + start, 2 * HD)
                total = ref[here, pl.ds(start, 2 * HD)].astype(F32) + other[there, span].astype(F32)
                payload[:, span] = total.astype(BF16)

        both = ends[here, :].astype(F32) + other[there, 2 * width :].astype(F32)
        payload[:, 2 * width :] = ends_of(both[:, :1] + both[:, HD // 2 : HD // 2 + 1])


def hidden_kernel(model_width, own, one, two, three, hidden):
    width = hidden.shape[1]

    def total(span):
        values = [ref[:, span].astype(F32) for ref in (own, one, two, three)]
        return values[0] + values[1] + values[2] + values[3]

    ends = total(pl.ds(2 * width, HD))
    squares = ends[:, :1] + ends[:, HD // 2 : HD // 2 + 1]
    factor = lax.rsqrt(squares / model_width + 1e-05)

    @pl.loop(0, width // (2 * HD))
    def _(step):
        start = pl.multiple_of(step * 2 * HD, 2 * HD)
        gate = total(pl.ds(start, 2 * HD)) * factor
        upper = total(pl.ds(width + start, 2 * HD)) * factor
        value = gate / (1.0 + jnp.exp(-gate)) * upper
        hidden[:, pl.ds(start, 2 * HD)] = value.astype(BF16)


def attend_slots(query_heads, key_rows, value_rows, cache_keys, cache_values, valid):
    slot_count, positions = cache_keys.shape[:2]
    kv_heads, groups = query_heads.shape[1:3]
    scaling = HD ** (-0.5)
    key_heads = cache_keys.reshape(slot_count, positions, kv_heads, HD)
    value_heads = cache_values.reshape(slot_count, positions, kv_heads, HD)
    scores = (
        jnp.einsum("bkgd,bckd->bkgc", query_heads, key_heads, preferred_element_type=F32) * scaling
    )
    new_score = (
        jnp.einsum("bkgd,bkd->bkg", query_heads, key_rows, preferred_element_type=F32) * scaling
    )
    inside = jnp.arange(positions)[None, :] < valid[:, None]
    scores = jnp.where(inside[:, None, None, :], scores, -jnp.inf)
    largest = jnp.maximum(jnp.max(scores, axis=-1), new_score)
    powers = jnp.exp(scores - largest[..., None])
    power_new = jnp.exp(new_score - largest)
    totals = jnp.sum(powers, axis=-1) + power_new
    weights = (powers / totals[..., None]).astype(BF16)
    weight_new = (power_new / totals).astype(BF16)
    context = jnp.einsum("bkgc,bckd->bkgd", weights, value_heads, preferred_element_type=F32)
    context = context + weight_new.astype(F32)[..., None] * value_rows.astype(F32)[:, :, None, :]
    return context.reshape(slot_count, kv_heads * groups * HD).astype(BF16)


def on_device(
    resid,
    queries,
    new_keys,
    new_values,
    cache_keys,
    cache_values,
    lengths,
    cache_slot,
    out_weight,
    norm_gain,
    gate_weight,
    up_weight,
    down_weight,
):
    index_gx = lax.axis_index("gx")
    index_yz = lax.axis_index("yz")
    count_yz = RING * RING
    count_gx = RING * CORES
    z, core = index_gx // CORES, index_gx % CORES
    x, y = index_yz // RING, index_yz % RING
    rows = resid.shape[0]
    width = resid.shape[1]
    per_device = cache_keys.shape[0]
    group_slots = per_device * count_yz
    block = rows // count_yz
    kv_heads = cache_keys.shape[2] // HD
    head_width = out_weight.shape[0]
    heads_here = head_width // HD
    new_width = new_keys.shape[1]

    slot_here = index_gx * group_slots + jnp.arange(group_slots, dtype=jnp.int32)
    routing = cache_slot[None, :] == slot_here[:, None]
    outgoing = jnp.concatenate(
        [pick(routing.astype(BF16), values) for values in (queries, new_keys, new_values)], axis=1
    )
    valid = jnp.sum(jnp.where(routing, lengths[None, :], 0), axis=1)
    valid_own = lax.dynamic_slice_in_dim(valid, index_yz * per_device, per_device)
    arrived = lax.all_to_all(outgoing, "yz", split_axis=0, concat_axis=0, tiled=True)
    arrived = arrived.reshape(count_yz, per_device, head_width + 2 * new_width)
    query_heads = (
        arrived[:, :, :head_width]
        .reshape(count_yz, per_device, heads_here, HD)
        .transpose(1, 0, 2, 3)
        .reshape(per_device, kv_heads, count_yz * heads_here // kv_heads, HD)
    )
    key_rows = (
        arrived[:, :, head_width : head_width + new_width]
        .transpose(1, 0, 2)
        .reshape(per_device, kv_heads, HD)
    )
    value_rows = (
        arrived[:, :, head_width + new_width :].transpose(1, 0, 2).reshape(per_device, kv_heads, HD)
    )
    context = attend_slots(query_heads, key_rows, value_rows, cache_keys, cache_values, valid_own)

    outgoing = context.reshape(per_device, count_yz, head_width).transpose(1, 0, 2)
    outgoing = jnp.broadcast_to(outgoing[None], (count_gx,) + outgoing.shape)
    all_columns = lax.all_to_all(
        outgoing.reshape(count_gx * count_yz, per_device, head_width),
        AXES,
        split_axis=0,
        concat_axis=0,
        tiled=True,
    ).reshape(rows, head_width)

    positions = jnp.arange(rows // TURNS, dtype=jnp.int32)
    piece = block // TURNS
    chunk = RING * piece
    half = chunk // CORES
    hidden_width = gate_weight.shape[1]
    far, near, inner = positions // chunk, (positions // piece) % RING, positions % piece

    def sum_first(values, weight):
        cuts = 2 if weight is down_weight else 1
        span = RING // cuts
        parts = {}
        for cut in range(cuts):
            start = cut * span * chunk
            total = pick(values[start : start + span * chunk], weight)
            for j in range(span):
                parts[cut * span + j] = total[j * chunk : (j + 1) * chunk]
        return add_up(parts[0], spread(send_first, parts))

    def rows_here(number):
        row_x = jnp.where(core == 0, x + far, x + near) % RING
        row_y = jnp.where(core == 0, y + near, y + far) % RING
        return (row_x * RING + row_y) * block + number * piece + inner

    every_row = jnp.concatenate([rows_here(number) for number in range(TURNS)])
    slot_of = jnp.sum(
        jnp.where(every_row[:, None] == jnp.arange(rows)[None, :], cache_slot[None, :], 0), axis=1
    )
    every_context = pick(one_hot_rows(slot_of, rows), all_columns)
    first_rows = jnp.concatenate([rows_here(number)[:chunk] for number in range(TURNS)])
    every_resid = pick(one_hot_rows(first_rows, rows), resid)

    def project(number):
        context_rows = every_context[number * RING * chunk : (number + 1) * RING * chunk]
        resid_rows = every_resid[number * chunk : (number + 1) * chunk]
        part = sum_first(context_rows, out_weight)
        others = collect(send_second, part.astype(BF16))[1:]
        payload, middle = local_kernel(
            middle_kernel,
            [
                jax.ShapeDtypeStruct((chunk, width + HD), BF16),
                jax.ShapeDtypeStruct((piece, width), BF16),
            ],
            part,
            *others,
            resid_rows,
            norm_gain[None, :],
        )
        return middle, jnp.concatenate(collect(send_first, payload), axis=0)

    def gate_and_up(blocks):
        target = positions[: RING * half] // half
        distance = jnp.zeros_like(target)
        for order_index, j in enumerate(FAR_FIRST):
            distance = jnp.where(target == order_index, j, distance)
        part_x = (z + distance) % RING
        inner_half = positions[: RING * half] % half

        def half_rows(part_core):
            part_y = part_core * (RING // CORES) + inner_half // piece
            source = jnp.where(core == 0, part_x * RING + part_y, part_y * RING + part_x)
            return source * piece + inner_half % piece

        source = jnp.concatenate([half_rows(1 - core), half_rows(core)])
        sorted_rows = pick(one_hot_rows(source, rows // TURNS), blocks)
        gate = pick(sorted_rows[:, :width], gate_weight)
        upper = pick(sorted_rows[:, :width], up_weight)
        ends = sorted_rows[:, width:]
        sums_width = 2 * hidden_width + HD
        (gift,) = local_kernel(
            gift_kernel,
            [jax.ShapeDtypeStruct((RING * half, sums_width), BF16)],
            gate,
            upper,
            ends,
        )
        payloads = local_kernel(
            pair_kernel,
            [jax.ShapeDtypeStruct((half, sums_width), BF16)] * RING,
            gate,
            upper,
            ends,
            send_core(gift),
        )
        return dict(zip(FAR_FIRST, payloads))

    def activate(own, others):
        (hidden,) = local_kernel(
            functools.partial(hidden_kernel, width * count_gx),
            [jax.ShapeDtypeStruct((half, hidden_width), BF16)],
            own,
            *others,
        )
        own_hidden = jnp.concatenate(collect(send_z, hidden), axis=0)
        return hidden, jnp.concatenate([own_hidden, send_core(own_hidden)], axis=0)

    def finish(middle, all_hidden):
        place_x = jnp.where(core == 0, far, near)
        place_y = jnp.where(core == 0, near, far)
        place_core = (place_y // (RING // CORES) + core) % CORES
        place_z = (place_x - z) % RING
        place_here = (
            (place_core * RING + place_z) * half + (place_y % (RING // CORES)) * piece + inner
        )
        hidden_rows = pick(one_hot_rows(place_here, rows // TURNS), all_hidden)
        part = sum_first(hidden_rows, down_weight)
        parts = {k: part[k * piece : (k + 1) * piece] for k in range(RING)}
        parts = {k: part if k == 0 else part.astype(BF16) for k, part in parts.items()}
        projected = add_up(parts[0], spread(send_second, parts))
        return (middle.astype(F32) + projected).astype(BF16)

    middles, blocks = zip(*[project(number) for number in range(TURNS)])
    parts = [gate_and_up(blocks[0])]
    for number in range(1, TURNS):
        parts.append(gate_and_up(blocks[number]))
    results = []
    for number in range(TURNS):
        own = parts[number][0]
        hidden, all_hidden = activate(own, spread(send_z, parts[number]))
        results.append(finish(middles[number], all_hidden))
    return jnp.concatenate(results, axis=0)


def solution(mesh):
    in_specs = (
        P(None, "gx"),
        P(None, "yz"),
        P(None, "yz"),
        P(None, "yz"),
        P(("gx", "yz"), None, None),
        P(("gx", "yz"), None, None),
        P(),
        P(),
        P("yz", "gx"),
        P("gx"),
        P("gx", "yz"),
        P("gx", "yz"),
        P("yz", "gx"),
    )
    out_specs = P("yz", "gx")
    return jax.shard_map(
        on_device, mesh=mesh, in_specs=in_specs, out_specs=out_specs, check_vma=False
    )
```
